32 devices in a mesh: gx: 4 (over z), gy: 8 (over y, x, core).
Axes of the slice: x: 2, y: 2, z: 4, core: 2. Of those that a mesh axis runs over, the one named last changes fastest.
Arguments:
- embeddings: bfloat16 [393216, 256], P(('gx', 'gy'))
- start: float32 [32, 393216], P(None, ('gx', 'gy'))
- requests: int32 [32, 8], P(('gx', 'gy')), may hold values from -1 to 23, as said below
- pairs: int32 [32, 40, 2], P(('gx', 'gy')), may hold values from 0 to 31, as said below
- counts: int32 [32], P(('gx', 'gy')), may hold values from 24 to 40, as said below
Outputs:
- spectral: float32 [32, 393216], P(None, ('gx', 'gy'))
The draws below stay inside these ranges and needn't reach their ends.
Inputs may be any that keep to these rules, and one draw needn't show every extreme that they name: requests[d, q] is -1 where q is d's own index along gy; every entry that is not -1 is used by some live slot of d. A live slot (a, s) has a < 24; if s < 24 then a <= s, else requests[d, s - 24] >= 0; every block of a device has a live slot (a, a); local pairs of one device are distinct; slots at or beyond counts[d] are (0, 0). counts[d] = 24 + (entries of requests[d] that are not -1) + (slots pairing two different blocks of d); in every gx group some device has all 40 slots live.
All inputs are finite; a program needn't handle non-finite values.
Results may differ from the reference program's by a relative error of at most 0.0046.
Values may be sent and summed in bfloat16 or wider, within the bound.
A program may use at most 192 MiB of HBM per device.

```python
import math
import jax
import jax.numpy as jnp
from jax import lax

D = 256
VECS = 32
BLK = 512
BLOCKS_DEV = 24
EXTRA = 9
ITERS = 2
ROW_DEV = 12288
ROWS = 393216
SLOTS = 40
N_GX = 4
N_GY = 8


def device_slots(key, wanted, extra_count):
    peer_count = wanted.shape[0]
    key_row, key_local, key_order = jax.random.split(key, 3)
    diag_ids = jnp.arange(BLOCKS_DEV, dtype=jnp.int32)
    remote_rows = jax.random.randint(key_row, (peer_count,), 0, BLOCKS_DEV, dtype=jnp.int32)
    remote_cols = BLOCKS_DEV + jnp.arange(peer_count, dtype=jnp.int32)
    candidate = jax.random.permutation(key_local, BLOCKS_DEV * BLOCKS_DEV).astype(jnp.int32)
    cand_row = candidate // BLOCKS_DEV
    cand_col = candidate % BLOCKS_DEV
    upper_first = jnp.argsort(jnp.where(cand_row < cand_col, 0, 1), stable=True)[:EXTRA]
    local_rows = cand_row[upper_first]
    local_cols = cand_col[upper_first]
    all_rows = jnp.concatenate([diag_ids, remote_rows, local_rows])
    all_cols = jnp.concatenate([diag_ids, remote_cols, local_cols])
    alive = jnp.concatenate([jnp.ones((BLOCKS_DEV,), bool), wanted, jnp.arange(EXTRA) < extra_count])
    entry_total = all_rows.shape[0]
    shuffle = jax.random.permutation(key_order, entry_total).astype(jnp.int32)
    order_key = jnp.where(alive, 0, entry_total) + shuffle
    slot_order = jnp.argsort(order_key)
    slot_total = entry_total - 1
    picked_live = alive[slot_order][:slot_total]
    rows_out = jnp.where(picked_live, all_rows[slot_order][:slot_total], 0)
    cols_out = jnp.where(picked_live, all_cols[slot_order][:slot_total], 0)
    return jnp.stack([rows_out, cols_out], axis=-1).astype(jnp.int32)


def plan(key):
    peer_count = SLOTS - BLOCKS_DEV - EXTRA + 1
    device_total = ROWS // ROW_DEV
    group_total = device_total // peer_count
    key_busy, key_want, key_pick, key_extra, key_slot = jax.random.split(key, 5)
    device = jnp.arange(device_total, dtype=jnp.int32)
    minor_index = device % peer_count
    major_index = device // peer_count
    crowded = minor_index == jax.random.randint(key_busy, (group_total,), 0, peer_count, dtype=jnp.int32)[major_index]
    peer_ids = jnp.arange(peer_count, dtype=jnp.int32)
    wanted = (jax.random.randint(key_want, (device_total, peer_count), 0, 2, dtype=jnp.int32) == 1) | crowded[:, None]
    wanted = wanted & (peer_ids[None, :] != minor_index[:, None])
    requests = jnp.where(wanted, jax.random.randint(key_pick, (device_total, peer_count), 0, BLOCKS_DEV, dtype=jnp.int32), -1)
    extra_count = jnp.where(crowded, EXTRA, jax.random.randint(key_extra, (device_total,), 0, EXTRA + 1, dtype=jnp.int32))
    counts = (BLOCKS_DEV + jnp.sum(wanted.astype(jnp.int32), axis=1) + extra_count).astype(jnp.int32)
    pairs = jax.vmap(device_slots)(jax.random.split(key_slot, device_total), wanted, extra_count)
    return (requests.astype(jnp.int32), pairs, counts)


def draw_requests(key, part):
    shared = plan(key)
    return shared[0]


def draw_pairs(key, part):
    shared = plan(key)
    return shared[1]


def draw_counts(key, part):
    shared = plan(key)
    return shared[2]


def draw_embeddings(key, part):
    key = jax.random.fold_in(key, 22)
    key_centre, key_voice, key_jitter, key_scale = jax.random.split(key, 4)
    voices = max(2, BLK // 32)
    centres = jax.random.normal(key_centre, (voices, D), jnp.float32)
    voice_ids = jax.random.randint(key_voice, (ROWS,), 0, voices, dtype=jnp.int32)
    jitter = jax.random.normal(key_jitter, (ROWS, D), jnp.float32)
    row_scale = jnp.exp(jax.random.uniform(key_scale, (ROWS, 1), jnp.float32, math.log(0.5), math.log(8.0)))
    return ((0.6 * centres[voice_ids] + 0.8 * jitter) * row_scale).astype(jnp.bfloat16)


def draw_start(key, part):
    key = jax.random.fold_in(key, 21)
    key_column, key_row, key_basis = jax.random.split(key, 3)
    column = jnp.exp(jax.random.uniform(key_column, (VECS, 1), jnp.float32, 0.0, math.log(10.0)))
    row_factor = jnp.exp(jax.random.uniform(key_row, (1, ROWS), jnp.float32, 0.0, math.log(10.0)))
    rising = jnp.exp(math.log(3.0) * jnp.arange(ROWS, dtype=jnp.float32) / ROWS)[None, :]
    basis = jax.random.normal(key_basis, (VECS, ROWS), jnp.float32)
    return (basis * column * row_factor * rising).astype(jnp.float32)


def setup_inputs(seed: int = 0) -> dict:
    splits = jax.random.split(jax.random.key(seed), 6)
    embeddings = draw_embeddings(jax.random.fold_in(splits[5], 71), 0)
    start = draw_start(jax.random.fold_in(splits[5], 71), 0)
    requests = draw_requests(jax.random.fold_in(splits[5], 71), 0)
    pairs = draw_pairs(jax.random.fold_in(splits[5], 71), 0)
    counts = draw_counts(jax.random.fold_in(splits[5], 71), 0)
    return {"embeddings": embeddings, "start": start, "requests": requests, "pairs": pairs, "counts": counts}


def normalize(raw_rows):
    values = raw_rows.astype(jnp.float32)
    scaled = values * lax.rsqrt(lax.optimization_barrier(jnp.sum(values * values, axis=-1, keepdims=True)) + 1e-06)
    return scaled.astype(jnp.bfloat16)

def make_tiles(left_rows, right_rows):
    product = jnp.einsum('srd,scd->src', left_rows.astype(jnp.float32), right_rows.astype(jnp.float32), precision=lax.Precision.HIGHEST)
    return (product * product * product).astype(jnp.bfloat16)

def apply_tiles(units, rounded, row_block, col_block, live_weight, twice):
    block_total = units.shape[0]
    vec_blocks = rounded.reshape(VECS, block_total, BLK).transpose(1, 0, 2)

    def device_pass(total, slot_data):
        rows_index, cols_index, live_row, live_col = slot_data
        tile_stack = make_tiles(units[rows_index], units[cols_index]).astype(jnp.float32)
        row_vecs = vec_blocks[rows_index].astype(jnp.float32)
        col_vecs = vec_blocks[cols_index].astype(jnp.float32)
        to_row = jnp.einsum('skc,src->skr', col_vecs, tile_stack, precision=lax.Precision.HIGHEST) * live_row[:, None, None]
        to_col = jnp.einsum('skr,src->skc', row_vecs, tile_stack, precision=lax.Precision.HIGHEST) * live_col[:, None, None]
        total = total.at[rows_index].add(to_row).at[cols_index].add(to_col)
        return (total, None)
    empty = jnp.zeros((block_total, VECS, BLK), jnp.float32)
    total = lax.scan(device_pass, empty, (row_block, col_block, live_weight, twice))[0]
    return total.transpose(1, 0, 2).reshape(VECS, block_total * BLK)

def orthonormalize(image):
    gram_matrix = jnp.dot(image.astype(jnp.float32), image.T.astype(jnp.float32), precision=lax.Precision.HIGHEST, preferred_element_type=jnp.float32)
    lower_factor = jnp.linalg.cholesky(gram_matrix / ROWS)
    return lax.linalg.triangular_solve(lower_factor, image, left_side=True, lower=True)

def reference(embeddings, start, requests, pairs, counts):
    device_total = N_GX * N_GY
    block_total = device_total * BLOCKS_DEV
    units = lax.map(normalize, embeddings.reshape(device_total, ROW_DEV, D)).reshape(block_total, BLK, D)
    device = jnp.arange(device_total, dtype=jnp.int32)[:, None]
    row_local = pairs[:, :, 0].astype(jnp.int32)
    col_local = pairs[:, :, 1].astype(jnp.int32)
    peer_slot = jnp.clip(col_local - BLOCKS_DEV, 0, N_GY - 1).astype(jnp.int32)
    peer_block = jnp.maximum(jnp.take_along_axis(requests, peer_slot, axis=1), 0).astype(jnp.int32)
    remote_block = (device // N_GY * N_GY + peer_slot) * BLOCKS_DEV + peer_block
    row_block = (device * BLOCKS_DEV + row_local).astype(jnp.int32)
    col_block = jnp.where(col_local < BLOCKS_DEV, device * BLOCKS_DEV + col_local, remote_block).astype(jnp.int32)
    slot_live = jnp.arange(SLOTS, dtype=jnp.int32)[None, :] < counts[:, None]
    live_weight = slot_live.astype(jnp.float32)
    twice = (slot_live & (row_block != col_block)).astype(jnp.float32)
    vectors = start
    for iteration in range(ITERS):
        image = apply_tiles(units, vectors.astype(jnp.bfloat16), row_block, col_block, live_weight, twice)
        vectors = orthonormalize(image)
    return vectors
```

```python
import functools

import jax
import jax.numpy as jnp
from jax import lax
from jax.experimental import pallas as pl
from jax.experimental.pallas import tpu as pltpu
from jax.sharding import PartitionSpec as P

D = 256
VECS = 32
BLK = 512
ITERS = 2
HALF = 256
MESH = pl.DeviceIdType.MESH
F32 = jnp.float32
BF16 = jnp.bfloat16


def normalize(raw_rows):
    values = raw_rows.astype(F32)
    scaled = values * lax.rsqrt(jnp.sum(values * values, axis=-1, keepdims=True) + 1e-06)
    return scaled.astype(BF16)


def dot_nn(a, b):
    return lax.dot_general(a, b, (((1,), (0,)), ((), ())), preferred_element_type=F32)


def dot_nt(a, b):
    return lax.dot_general(a, b, (((1,), (1,)), ((), ())), preferred_element_type=F32)


def split3(x):
    high = x.astype(BF16)
    rest = x - high.astype(F32)
    mid = rest.astype(BF16)
    low = (rest - mid.astype(F32)).astype(BF16)
    return jnp.concatenate([high, mid, low], axis=0)


def inverse_factor(gram):
    row = lax.broadcasted_iota(jnp.int32, (VECS, 4 * VECS), 0)
    lane = lax.broadcasted_iota(jnp.int32, (VECS, 4 * VECS), 1)
    eye = ((lane % VECS) == row).astype(F32)
    work = jnp.concatenate([eye[:, : 3 * VECS], gram], axis=1)
    for k in range(VECS):
        pivot_row = work[k : k + 1, :]
        column = work[:, 3 * VECS + k : 3 * VECS + k + 1]
        pivot = work[k : k + 1, 3 * VECS + k : 3 * VECS + k + 1]
        factor = jnp.where(row[:, :1] > k, column / pivot, 0.0)
        work = work - factor * pivot_row
    pivots = jnp.sum(jnp.where(lane == row + 3 * VECS, work, 0.0), axis=1, keepdims=True)
    return work[:, : 3 * VECS] * lax.rsqrt(pivots)


def kernel(
    peers, groups, extra, stash, rows_all,
    table, req, emb, start, out,
    req_all, wanted, unit, near_w, tiles, image, split,
    rows_send, rows_far, w_send, w_far, ex_row, ex_col, far_row, ret_send, ret_far,
    gram_y, gram_x,
    local_sem, req_s, req_r, rows_s, rows_r, w_s, w_r, ret_s, ret_r, gy_s, gy_r, gx_s, gx_r,
):
    blocks = emb.shape[0]
    gx = lax.axis_index("gx")
    me = lax.axis_index("gy")

    def ahead(o):
        return lax.rem(me + o, peers)

    def behind(o):
        return lax.rem(me + peers - o, peers)

    def remote(src, dst, s_sem, r_sem, target):
        return pltpu.make_async_remote_copy(
            src_ref=src, dst_ref=dst, send_sem=s_sem, recv_sem=r_sem,
            device_id=target, device_id_type=MESH,
        )

    def req_copy(o):
        return remote(req, req_all.at[o - 1], req_s.at[o - 1], req_r.at[o - 1], (gx, ahead(o)))

    def rows_copy(o):
        return remote(
            rows_send.at[o - 1], rows_far.at[o - 1], rows_s.at[o - 1], rows_r.at[o - 1],
            (gx, behind(o)),
        )

    def w_copy(it, o):
        return remote(
            w_send.at[it, o - 1], w_far.at[it, o - 1], w_s.at[it, o - 1], w_r.at[it, o - 1],
            (gx, behind(o)),
        )

    def ret_copy(it, o):
        return remote(
            ret_send.at[it, o - 1], ret_far.at[it, o - 1], ret_s.at[it, o - 1],
            ret_r.at[it, o - 1], (gx, ahead(o)),
        )

    def gy_copy(it, o):
        return remote(
            gram_y.at[it, me], gram_y.at[it, me], gy_s.at[it, o - 1], gy_r.at[it, o - 1],
            (gx, ahead(o)),
        )

    def gx_copy(it, o):
        return remote(
            gram_x.at[it, gx], gram_x.at[it, gx], gx_s.at[it, o - 1], gx_r.at[it, o - 1],
            (lax.rem(gx + o, groups), me),
        )

    def each(count, body, first=0, unroll=1):
        def step(i, carry):
            body(i)
            return carry

        lax.fori_loop(first, count, step, 0, unroll=unroll)

    def block_columns(b):
        return pl.ds(pl.multiple_of(b * BLK, BLK), BLK)

    barrier = pltpu.get_barrier_semaphore()
    each(
        peers,
        lambda o: pl.semaphore_signal(barrier, inc=1, device_id=(gx, ahead(o)), device_id_type=MESH),
        1,
    )
    each(
        groups,
        lambda o: pl.semaphore_signal(
            barrier, inc=1, device_id=(lax.rem(gx + o, groups), me), device_id_type=MESH
        ),
        1,
    )
    pl.semaphore_wait(barrier, peers + groups - 2)

    each(peers, lambda o: req_copy(o).start(), 1)

    def round_start(b):
        near_w[b] = start[:, block_columns(b)].astype(BF16)

    each(blocks, round_start, unroll=2)

    each(peers, lambda o: req_copy(o).wait(), 1)
    to_scalar = pltpu.make_async_copy(req_all, wanted, local_sem)
    to_scalar.start()
    to_scalar.wait()

    def send_w(it):
        def body(o):
            index = jnp.maximum(wanted[o - 1, 0, me], 0)
            w_send[it, o - 1] = near_w[index]
            w_copy(it, o).start()

        each(peers, body, 1)

    send_w(0)

    def send_rows(o):
        index = jnp.maximum(wanted[o - 1, 0, me], 0)
        rows_send[o - 1] = normalize(emb[index])
        rows_copy(o).start()

    each(peers, send_rows, 1)

    def build(slot, left, right):
        for part in range(BLK // HALF):
            span = pl.ds(part * HALF, HALF)
            product = dot_nt(left[part * HALF : (part + 1) * HALF], right)
            tiles[slot, span, :] = (product * product * product).astype(BF16)

    for it in range(ITERS):
        fresh = it == 0 or not stash

        def diagonal(b):
            slot = b if stash else 0
            if it == 0:
                unit[b] = normalize(emb[b])
            if fresh:
                rows = unit[b]
                build(slot, rows, rows)
            image[b] = dot_nn(near_w[b], tiles[slot])

        each(blocks, diagonal, unroll=2)

        def local_pair(e):
            slot = blocks + e if stash else 0
            left = jnp.maximum(table[peers + e], 0)
            right = jnp.maximum(table[peers + extra + e], 0)
            if fresh:
                build(slot, unit[left], unit[right])
            ex_row[e] = dot_nt(near_w[right], tiles[slot])
            ex_col[e] = dot_nn(near_w[left], tiles[slot])

        each(extra, local_pair)

        def add_local(b):
            total = image[b]
            for e in range(extra):
                total += (table[peers + e] == b).astype(F32) * ex_row[e]
                total += (table[peers + extra + e] == b).astype(F32) * ex_col[e]
            image[b] = total

        each(blocks, add_local)

        def far_pair(o):
            slot = blocks + extra + o - 1 if stash else 0
            left = jnp.maximum(table[ahead(o)], 0)
            if it == 0:
                rows_copy(o).wait_recv()
            w_copy(it, o).wait_recv()
            if fresh:
                build(slot, unit[left], rows_far[o - 1])
            ret_send[it, o - 1] = dot_nn(near_w[left], tiles[slot])
            ret_copy(it, o).start()
            far_row[o - 1] = dot_nt(w_far[it, o - 1], tiles[slot])

        each(peers, far_pair, 1)

        def add_far(b):
            total = image[b]
            for o in range(1, peers):
                total += (table[ahead(o)] == b).astype(F32) * far_row[o - 1]
            image[b] = total

        each(blocks, add_far)

        each(peers, lambda o: ret_copy(it, o).wait_recv(), 1)

        def add_returned(b):
            total = image[b]
            for o in range(1, peers):
                total += (wanted[o - 1, 0, me] == b).astype(F32) * ret_far[it, o - 1]
            split[:, block_columns(b)] = split3(total)

        each(blocks, add_returned)

        parts = split[...]
        products = dot_nt(parts, parts)
        products = products[:VECS] + products[VECS : 2 * VECS] + products[2 * VECS :]
        gram = products[:, :VECS] + products[:, VECS : 2 * VECS] + products[:, 2 * VECS :]
        gram_y[it, me] = jnp.concatenate([gram[8 * i : 8 * i + 8] for i in range(4)], axis=1)
        each(peers, lambda o: gy_copy(it, o).start(), 1)

        def gy_wait(o):
            remote(
                gram_y.at[it, me], gram_y.at[it, behind(o)], gy_s.at[it, o - 1],
                gy_r.at[it, o - 1], (gx, ahead(o)),
            ).wait_recv()

        each(peers, gy_wait, 1)
        each(peers, lambda o: gy_copy(it, o).wait_send(), 1)
        gram_x[it, gx] = jnp.sum(gram_y[it], axis=0)
        each(groups, lambda o: gx_copy(it, o).start(), 1)

        def gx_wait(o):
            remote(
                gram_x.at[it, gx], gram_x.at[it, lax.rem(gx + groups - o, groups)],
                gx_s.at[it, o - 1], gx_r.at[it, o - 1], (lax.rem(gx + o, groups), me),
            ).wait_recv()

        each(groups, gx_wait, 1)
        each(groups, lambda o: gx_copy(it, o).wait_send(), 1)
        packed = jnp.sum(gram_x[it], axis=0)
        gram = jnp.concatenate(
            [packed[:, VECS * i : VECS * (i + 1)] for i in range(4)], axis=0
        )
        factor = split3(inverse_factor(gram / rows_all))

        def apply_factor(b):
            triple = dot_nn(factor, split[:, block_columns(b)])
            result = triple[:VECS] + triple[VECS : 2 * VECS] + triple[2 * VECS :]
            if it < ITERS - 1:
                near_w[b] = result.astype(BF16)
            else:
                out[:, block_columns(b)] = result

        each(blocks, apply_factor, unroll=2)
        if it < ITERS - 1:
            send_w(it + 1)

    each(peers, lambda o: req_copy_done(o, rows_copy, w_copy, ret_copy), 1)


def req_copy_done(o, rows_copy, w_copy, ret_copy):
    rows_copy(o).wait_send()
    for it in range(ITERS):
        w_copy(it, o).wait_send()
        ret_copy(it, o).wait_send()


def slot_table(pairs, counts, blocks, peers, extra):
    slots = pairs.shape[1]
    row_slot, col_slot = pairs[0, :, 0], pairs[0, :, 1]
    index = jnp.arange(slots, dtype=jnp.int32)
    live = index < counts[0]
    far = live[None, :] & (col_slot[None, :] == blocks + jnp.arange(peers, dtype=jnp.int32)[:, None])
    local = live & (col_slot < blocks) & (row_slot != col_slot)
    before = jnp.sum((local[None, :] & (index[None, :] < index[:, None])).astype(jnp.int32), axis=1)
    near = local[None, :] & (before[None, :] == jnp.arange(extra, dtype=jnp.int32)[:, None])

    def pick(mask, values):
        return jnp.sum(jnp.where(mask, values[None, :] + 1, 0), axis=1) - 1

    return jnp.concatenate([pick(far, row_slot), pick(near, row_slot), pick(near, col_slot)])


def per_device(embeddings, start, requests, pairs, counts):
    peers = lax.axis_size("gy")
    groups = lax.axis_size("gx")
    row_total = embeddings.shape[0]
    blocks = row_total // BLK
    extra = pairs.shape[1] - blocks - (peers - 1)
    stash = peers <= 8
    tile_count = blocks + extra + peers - 1 if stash else 1
    table = slot_table(pairs, counts, blocks, peers, extra)
    req = jnp.pad(requests, ((0, 7), (0, 128 - peers)), constant_values=-1)
    hops = peers - 1
    dma = pltpu.SemaphoreType.DMA
    vmem = pl.BlockSpec(memory_space=pltpu.VMEM)
    return pl.pallas_call(
        functools.partial(kernel, peers, groups, extra, stash, float(row_total * groups * peers)),
        out_shape=jax.ShapeDtypeStruct(start.shape, F32),
        in_specs=[pl.BlockSpec(memory_space=pltpu.SMEM), vmem, vmem, vmem],
        out_specs=vmem,
        scratch_shapes=[
            pltpu.VMEM((hops, 8, 128), jnp.int32),
            pltpu.SMEM((hops, 8, 128), jnp.int32),
            pltpu.VMEM((blocks, BLK, D), BF16),
            pltpu.VMEM((blocks, VECS, BLK), BF16),
            pltpu.VMEM((tile_count, BLK, BLK), BF16),
            pltpu.VMEM((blocks, VECS, BLK), F32),
            pltpu.VMEM((3 * VECS, row_total), BF16),
            pltpu.VMEM((hops, BLK, D), BF16),
            pltpu.VMEM((hops, BLK, D), BF16),
            pltpu.VMEM((ITERS, hops, VECS, BLK), BF16),
            pltpu.VMEM((ITERS, hops, VECS, BLK), BF16),
            pltpu.VMEM((extra, VECS, BLK), F32),
            pltpu.VMEM((extra, VECS, BLK), F32),
            pltpu.VMEM((hops, VECS, BLK), F32),
            pltpu.VMEM((ITERS, hops, VECS, BLK), F32),
            pltpu.VMEM((ITERS, hops, VECS, BLK), F32),
            pltpu.VMEM((ITERS, peers, 8, 128), F32),
            pltpu.VMEM((ITERS, groups, 8, 128), F32),
            dma,
            dma((hops,)),
            dma((hops,)),
            dma((hops,)),
            dma((hops,)),
            dma((ITERS, hops)),
            dma((ITERS, hops)),
            dma((ITERS, hops)),
            dma((ITERS, hops)),
            dma((ITERS, hops)),
            dma((ITERS, hops)),
            dma((ITERS, groups - 1)),
            dma((ITERS, groups - 1)),
        ],
        compiler_params=pltpu.CompilerParams(
            collective_id=0, has_side_effects=True, vmem_limit_bytes=60 * 1024 * 1024
        ),
    )(table, req, embeddings.reshape(blocks, BLK, D), start)


def solution(mesh):
    return jax.shard_map(
        per_device,
        mesh=mesh,
        in_specs=(
            P(("gx", "gy"), None),
            P(None, ("gx", "gy")),
            P(("gx", "gy"), None),
            P(("gx", "gy"), None, None),
            P(("gx", "gy")),
        ),
        out_specs=P(None, ("gx", "gy")),
        check_vma=False,
    )
```

```python
import functools

import jax
import jax.numpy as jnp
from jax import lax
from jax.experimental import pallas as pl
from jax.experimental.pallas import tpu as pltpu
from jax.sharding import PartitionSpec as P

D = 256
VECS = 32
BLK = 512
ITERS = 2
HALF = 256
MESH = pl.DeviceIdType.MESH
F32 = jnp.float32
BF16 = jnp.bfloat16


def normalize(raw_rows):
    values = raw_rows.astype(F32)
    scaled = values * lax.rsqrt(jnp.sum(values * values, axis=-1, keepdims=True) + 1e-06)
    return scaled.astype(BF16)


def dot_nn(a, b):
    return lax.dot_general(a, b, (((1,), (0,)), ((), ())), preferred_element_type=F32)


def dot_nt(a, b):
    return lax.dot_general(a, b, (((1,), (1,)), ((), ())), preferred_element_type=F32)


def split3(x):
    high = x.astype(BF16)
    rest = x - high.astype(F32)
    mid = rest.astype(BF16)
    low = (rest - mid.astype(F32)).astype(BF16)
    return jnp.concatenate([high, mid, low], axis=0)


def inverse_factor(gram):
    row = lax.broadcasted_iota(jnp.int32, (VECS, 4 * VECS), 0)
    lane = lax.broadcasted_iota(jnp.int32, (VECS, 4 * VECS), 1)
    eye = ((lane % VECS) == row).astype(F32)
    work = jnp.concatenate([eye[:, : 3 * VECS], gram], axis=1)
    shape = (VECS, 4 * VECS)
    base = 3 * VECS
    for k in range(0, VECS, 2):
        first = jnp.broadcast_to(work[:, base + k : base + k + 1], shape)
        second = jnp.broadcast_to(work[:, base + k + 1 : base + k + 2], shape)
        row0, row1 = work[k : k + 1, :], work[k + 1 : k + 2, :]
        scale = 1.0 / first[k : k + 1, :]
        ratio = first[k + 1 : k + 2, :] * scale
        below = row1 - ratio * row0
        second = second - first * ratio
        inverse = 1.0 / second[k + 1 : k + 2, :]
        work = (
            work
            - jnp.where(row > k, first, 0.0) * (scale * row0)
            - jnp.where(row > k + 1, second, 0.0) * (inverse * below)
        )
    pivots = jnp.sum(jnp.where(lane == row + 3 * VECS, work, 0.0), axis=1, keepdims=True)
    return work[:, : 3 * VECS] * lax.rsqrt(pivots)


def kernel(
    peers, groups, extra, stash, rows_all,
    pairs, counts, requests, emb_hbm, start_hbm, image_hbm, last_factor,
    table, emb, start, req, req_all, wanted, unit, near_w, tiles, image, split,
    rows_send, rows_far, w_send, w_far, ex_row, ex_col, far_row, ret_send, ret_far,
    gram_y, gram_x,
    local_sem, emb_sem, start_sem, image_sem, req_s, req_r, rows_s, rows_r, w_s, w_r, ret_s, ret_r, gy_s, gy_r, gx_s, gx_r,
):
    blocks = emb.shape[0]
    gx = lax.axis_index("gx")
    me = lax.axis_index("gy")

    def ahead(o):
        return lax.rem(me + o, peers)

    def behind(o):
        return lax.rem(me + peers - o, peers)

    def remote(src, dst, s_sem, r_sem, target):
        return pltpu.make_async_remote_copy(
            src_ref=src, dst_ref=dst, send_sem=s_sem, recv_sem=r_sem,
            device_id=target, device_id_type=MESH,
        )

    def req_copy(o):
        return remote(req, req_all.at[o - 1], req_s.at[o - 1], req_r.at[o - 1], (gx, ahead(o)))

    def rows_copy(o):
        return remote(
            rows_send.at[o - 1], rows_far.at[o - 1], rows_s.at[o - 1], rows_r.at[o - 1],
            (gx, behind(o)),
        )

    def w_copy(it, o):
        return remote(
            w_send.at[it, o - 1], w_far.at[it, o - 1], w_s.at[it, o - 1], w_r.at[it, o - 1],
            (gx, behind(o)),
        )

    def ret_copy(it, o):
        return remote(
            ret_send.at[it, o - 1], ret_far.at[it, o - 1], ret_s.at[it, o - 1],
            ret_r.at[it, o - 1], (gx, ahead(o)),
        )

    def gy_copy(it, o):
        return remote(
            gram_y.at[it, me], gram_y.at[it, me], gy_s.at[it, o - 1], gy_r.at[it, o - 1],
            (gx, ahead(o)),
        )

    def gx_copy(it, o):
        return remote(
            gram_x.at[it, gx], gram_x.at[it, gx], gx_s.at[it, o - 1], gx_r.at[it, o - 1],
            (lax.rem(gx + o, groups), me),
        )

    def each(count, body, first=0, unroll=1):
        def step(i, carry):
            body(i)
            return carry

        lax.fori_loop(first, count, step, 0, unroll=unroll)

    def block_columns(b):
        return pl.ds(pl.multiple_of(b * BLK, BLK), BLK)

    start_in = pltpu.make_async_copy(start_hbm, start, start_sem)
    emb_in = pltpu.make_async_copy(emb_hbm, emb, emb_sem)
    start_in.start()
    emb_in.start()
    req[...] = jnp.full(req.shape, -1, jnp.int32)
    req[0:1, 0:peers] = requests[...]

    barrier = pltpu.get_barrier_semaphore()
    each(
        peers,
        lambda o: pl.semaphore_signal(barrier, inc=1, device_id=(gx, ahead(o)), device_id_type=MESH),
        1,
    )
    each(
        groups,
        lambda o: pl.semaphore_signal(
            barrier, inc=1, device_id=(lax.rem(gx + o, groups), me), device_id_type=MESH
        ),
        1,
    )
    pl.semaphore_wait(barrier, peers + groups - 2)

    each(peers, lambda o: req_copy(o).start(), 1)

    fill_table(table, pairs, counts, blocks, peers, extra)
    start_in.wait()

    def round_start(b):
        near_w[b] = start[:, block_columns(b)].astype(BF16)

    each(blocks, round_start, unroll=2)

    each(peers, lambda o: req_copy(o).wait(), 1)
    to_scalar = pltpu.make_async_copy(req_all, wanted, local_sem)
    to_scalar.start()
    to_scalar.wait()

    def send_w(it):
        def body(o):
            index = jnp.maximum(wanted[o - 1, 0, me], 0)
            w_send[it, o - 1] = near_w[index]
            w_copy(it, o).start()

        each(peers, body, 1)

    send_w(0)
    emb_in.wait()

    def send_rows(o):
        index = jnp.maximum(wanted[o - 1, 0, me], 0)
        rows_send[o - 1] = normalize(emb[index])
        rows_copy(o).start()

    each(peers, send_rows, 1)

    def build(slot, left, right):
        for part in range(BLK // HALF):
            span = pl.ds(part * HALF, HALF)
            product = dot_nt(left[part * HALF : (part + 1) * HALF], right)
            tiles[slot, span, :] = (product * product * product).astype(BF16)

    for it in range(ITERS):
        fresh = it == 0 or not stash

        def diagonal(b):
            slot = b if stash else 0
            if it == 0:
                unit[b] = normalize(emb[b])
            if fresh:
                rows = unit[b]
                build(slot, rows, rows)
            image[b] = dot_nn(near_w[b], tiles[slot])

        each(blocks, diagonal, unroll=2)

        def local_pair(e):
            slot = blocks + e if stash else 0
            left = jnp.maximum(table[peers + e], 0)
            right = jnp.maximum(table[peers + extra + e], 0)
            if fresh:
                build(slot, unit[left], unit[right])
            ex_row[e] = dot_nt(near_w[right], tiles[slot])
            ex_col[e] = dot_nn(near_w[left], tiles[slot])

        if it == 0:
            each(extra, local_pair)

        def far_pair(o):
            slot = blocks + extra + o - 1 if stash else 0
            left = jnp.maximum(table[ahead(o)], 0)
            if it == 0:
                rows_copy(o).wait_recv()
            w_copy(it, o).wait_recv()
            if fresh:
                build(slot, unit[left], rows_far[o - 1])
            ret_send[it, o - 1] = dot_nn(near_w[left], tiles[slot])
            ret_copy(it, o).start()
            far_row[o - 1] = dot_nt(w_far[it, o - 1], tiles[slot])

        each(peers, far_pair, 1)

        if it > 0:
            each(extra, local_pair)

        def add_own(b):
            total = image[b]
            for e in range(extra):
                total += (table[peers + e] == b).astype(F32) * ex_row[e]
                total += (table[peers + extra + e] == b).astype(F32) * ex_col[e]
            for o in range(1, peers):
                total += (table[ahead(o)] == b).astype(F32) * far_row[o - 1]
            image[b] = total

        each(blocks, add_own)

        each(peers, lambda o: ret_copy(it, o).wait_recv(), 1)

        def add_returned(b):
            total = image[b]
            for o in range(1, peers):
                total += (wanted[o - 1, 0, me] == b).astype(F32) * ret_far[it, o - 1]
            split[:, block_columns(b)] = split3(total)
            if it == ITERS - 1:
                image[b] = total

        each(blocks, add_returned)

        if it == ITERS - 1:
            pltpu.make_async_copy(image, image_hbm, image_sem).start()
        parts = split[...]
        products = dot_nt(parts, parts)
        products = products[:VECS] + products[VECS : 2 * VECS] + products[2 * VECS :]
        gram = products[:, :VECS] + products[:, VECS : 2 * VECS] + products[:, 2 * VECS :]
        gram_y[it, me] = jnp.concatenate([gram[8 * i : 8 * i + 8] for i in range(4)], axis=1)
        each(peers, lambda o: gy_copy(it, o).start(), 1)

        def gy_wait(o):
            remote(
                gram_y.at[it, me], gram_y.at[it, behind(o)], gy_s.at[it, o - 1],
                gy_r.at[it, o - 1], (gx, ahead(o)),
            ).wait_recv()

        each(peers, gy_wait, 1)
        gram_x[it, gx] = jnp.sum(gram_y[it], axis=0)
        each(groups, lambda o: gx_copy(it, o).start(), 1)

        def gx_wait(o):
            remote(
                gram_x.at[it, gx], gram_x.at[it, lax.rem(gx + groups - o, groups)],
                gx_s.at[it, o - 1], gx_r.at[it, o - 1], (lax.rem(gx + o, groups), me),
            ).wait_recv()

        each(groups, gx_wait, 1)
        packed = jnp.sum(gram_x[it], axis=0)
        gram = jnp.concatenate(
            [packed[:, VECS * i : VECS * (i + 1)] for i in range(4)], axis=0
        )
        factor = split3(inverse_factor(gram / rows_all))

        if it == ITERS - 1:
            last_factor[...] = factor
        else:

            def apply_factor(b):
                near_w[b] = apply_split(factor, split[:, block_columns(b)]).astype(BF16)

            each(blocks, apply_factor, unroll=2)
            send_w(it + 1)

    def finish(o):
        rows_copy(o).wait_send()
        for it in range(ITERS):
            w_copy(it, o).wait_send()
            ret_copy(it, o).wait_send()
            gy_copy(it, o).wait_send()

    def finish_x(o):
        for it in range(ITERS):
            gx_copy(it, o).wait_send()

    each(peers, finish, 1)
    each(groups, finish_x, 1)
    pltpu.make_async_copy(image, image_hbm, image_sem).wait()


def apply_split(factor, parts):
    triple = dot_nn(factor, parts)
    return triple[:VECS] + triple[VECS : 2 * VECS] + triple[2 * VECS :]


def last_kernel(factor, image, out):
    for b in range(image.shape[0]):
        out[:, b * BLK : (b + 1) * BLK] = apply_split(factor[...], split3(image[b]))


def fill_table(table, pairs, counts, blocks, peers, extra):
    live_count = counts[0]

    def step(k, carry):
        seen, far, rows, cols = carry
        r, s = pairs[0, 0, k], pairs[0, 1, k]
        s = jnp.where(k < live_count, s, -1)
        local = (s >= 0) & (s < blocks) & (r != s)
        place = jnp.where(local, seen, -1)
        far = tuple(jnp.where(s == blocks + q, r, far[q]) for q in range(peers))
        rows = tuple(jnp.where(place == e, r, rows[e]) for e in range(extra))
        cols = tuple(jnp.where(place == e, s, cols[e]) for e in range(extra))
        return seen + local.astype(jnp.int32), far, rows, cols

    none = jnp.int32(-1)
    _, far, rows, cols = lax.fori_loop(
        0, pairs.shape[2], step, (jnp.int32(0), (none,) * peers, (none,) * extra, (none,) * extra)
    )
    for index, value in enumerate(far + rows + cols):
        table[index] = value


def per_device(embeddings, start, requests, pairs, counts):
    peers = lax.axis_size("gy")
    groups = lax.axis_size("gx")
    row_total = embeddings.shape[0]
    blocks = row_total // BLK
    extra = pairs.shape[1] - blocks - (peers - 1)
    stash = peers <= 8
    tile_count = blocks + extra + peers - 1 if stash else 1
    hops = peers - 1
    dma = pltpu.SemaphoreType.DMA
    vmem = pl.BlockSpec(memory_space=pltpu.VMEM)
    smem = pl.BlockSpec(memory_space=pltpu.SMEM)
    hbm = pl.BlockSpec(memory_space=pl.ANY)
    image, factor = pl.pallas_call(
        functools.partial(kernel, peers, groups, extra, stash, float(row_total * groups * peers)),
        out_shape=(
            jax.ShapeDtypeStruct((blocks, VECS, BLK), F32),
            jax.ShapeDtypeStruct((3 * VECS, 3 * VECS), BF16),
        ),
        in_specs=[smem, smem, vmem, hbm, hbm],
        out_specs=(hbm, vmem),
        scratch_shapes=[
            pltpu.SMEM((peers + 2 * extra,), jnp.int32),
            pltpu.VMEM((blocks, BLK, D), BF16),
            pltpu.VMEM(start.shape, F32),
            pltpu.VMEM((8, 128), jnp.int32),
            pltpu.VMEM((hops, 8, 128), jnp.int32),
            pltpu.SMEM((hops, 8, 128), jnp.int32),
            pltpu.VMEM((blocks, BLK, D), BF16),
            pltpu.VMEM((blocks, VECS, BLK), BF16),
            pltpu.VMEM((tile_count, BLK, BLK), BF16),
            pltpu.VMEM((blocks, VECS, BLK), F32),
            pltpu.VMEM((3 * VECS, row_total), BF16),
            pltpu.VMEM((hops, BLK, D), BF16),
            pltpu.VMEM((hops, BLK, D), BF16),
            pltpu.VMEM((ITERS, hops, VECS, BLK), BF16),
            pltpu.VMEM((ITERS, hops, VECS, BLK), BF16),
            pltpu.VMEM((extra, VECS, BLK), F32),
            pltpu.VMEM((extra, VECS, BLK), F32),
            pltpu.VMEM((hops, VECS, BLK), F32),
            pltpu.VMEM((ITERS, hops, VECS, BLK), F32),
            pltpu.VMEM((ITERS, hops, VECS, BLK), F32),
            pltpu.VMEM((ITERS, peers, 8, 128), F32),
            pltpu.VMEM((ITERS, groups, 8, 128), F32),
            dma,
            dma,
            dma,
            dma,
            dma((hops,)),
            dma((hops,)),
            dma((hops,)),
            dma((hops,)),
            dma((ITERS, hops)),
            dma((ITERS, hops)),
            dma((ITERS, hops)),
            dma((ITERS, hops)),
            dma((ITERS, hops)),
            dma((ITERS, hops)),
            dma((ITERS, groups - 1)),
            dma((ITERS, groups - 1)),
        ],
        compiler_params=pltpu.CompilerParams(
            collective_id=0, has_side_effects=True, vmem_limit_bytes=60 * 1024 * 1024
        ),
    )(pairs.swapaxes(1, 2), counts, requests, embeddings.reshape(blocks, BLK, D), start)
    turn = next(n for n in (6, 4, 3, 2, 1) if blocks % n == 0)
    return pl.pallas_call(
        last_kernel,
        out_shape=jax.ShapeDtypeStruct(start.shape, F32),
        grid=(blocks // turn,),
        in_specs=[
            pl.BlockSpec((3 * VECS, 3 * VECS), lambda i: (0, 0)),
            pl.BlockSpec((turn, VECS, BLK), lambda i: (i, 0, 0)),
        ],
        out_specs=pl.BlockSpec((VECS, turn * BLK), lambda i: (0, i)),
        compiler_params=pltpu.CompilerParams(vmem_limit_bytes=60 * 1024 * 1024),
    )(factor, image)


def solution(mesh):
    return jax.shard_map(
        per_device,
        mesh=mesh,
        in_specs=(
            P(("gx", "gy"), None),
            P(None, ("gx", "gy")),
            P(("gx", "gy"), None),
            P(("gx", "gy"), None, None),
            P(("gx", "gy")),
        ),
        out_specs=P(None, ("gx", "gy")),
        check_vma=False,
    )
```
